256 devices in a mesh: dp: 8 (over y, core), tensor: 32 (over x, z).
Axes of the slice: x: 4, y: 4, z: 8, core: 2. Of those that a mesh axis runs over, the one named last changes fastest.
Arguments:
- out_grad: bfloat16 [4096, 4096], P(('dp', 'tensor')), may hold values from -6 to 6
- gate_pre: bfloat16 [4096, 16384], P('dp', 'tensor'), may hold values from -6 to 6
- up_pre: bfloat16 [4096, 16384], P('dp', 'tensor'), may hold values from -6 to 6
- gate_codes: int32 [1024, 16384], P(None, 'tensor'), may hold values from 0 to 65280
- up_codes: int32 [1024, 16384], P(None, 'tensor'), may hold values from 0 to 65280
- down_codes: int32 [16384, 1024], P('tensor'), may hold values from 0 to 65280
- gate_scale: float32 [32, 16384], P(None, 'tensor'), may hold values from 0.00171875 to 0.006875
- up_scale: float32 [32, 16384], P(None, 'tensor'), may hold values from 0.00171875 to 0.006875
- down_scale: float32 [128, 4096], P('tensor'), may hold values from 0.000859375 to 0.0034375
- weak_weight: bfloat16 [1024, 4096], P('tensor'), may hold values from -0.125 to 0.125
- weak_index: int32 [1024], P('tensor'), may hold values from -1 to 511, as said below
Outputs:
- in_grad: bfloat16 [4096, 4096], P(('dp', 'tensor'))
- weak_grad: float32 [1024, 4096], P('tensor', 'dp')
The draws below stay inside these ranges and needn't reach their ends.
Inputs may be any that keep to these rules, and one draw needn't show every extreme that they name: `weak_index`: slot s belongs to tensor rank s // 32. A rank's live slots come first and hold distinct hidden units of that rank, counted from 0; its other slots hold -1. Counts of live slots differ from rank to rank, and some rank has all 32 slots live.
All inputs are finite; a program needn't handle non-finite values.
Results may differ from the reference program's by a relative error of at most 0.017.
Values may be sent and summed in bfloat16 or wider, within the bound.
No kernel may reach another device: no remote copies, remote signals or barrier semaphores. Data moves between devices by JAX's collectives and lax.ppermute only.
A program may use at most 128 MiB of HBM per device.

```python
import math
import jax
import jax.numpy as jnp

D = 4096
FF = 16384
GROUP = 128
WMAX = 32
TOKENS = 4096
FF_RANK = 512
WEAK_SLOTS = 1024


def pick_units(unit_key):
    return jax.random.permutation(unit_key, FF_RANK - 1)[:WMAX]


def draw_weak_index(key, part):
    rank_count = WEAK_SLOTS // WMAX
    key_count, key_full, key_units = jax.random.split(key, 3)
    counts = jax.random.randint(key_count, (rank_count,), 1, WMAX // 2 + 1)
    full_rank = jax.random.randint(key_full, (), 0, rank_count)
    is_full = jnp.arange(rank_count) == full_rank
    counts = jnp.where(is_full, WMAX, counts)
    unit_order = jax.vmap(pick_units)(jax.random.split(key_units, rank_count))
    slot_number = jnp.arange(WMAX)[None, :]
    first_slot = (slot_number == 0) & is_full[:, None]
    unit_order = jnp.where(first_slot, FF_RANK - 1, unit_order)
    chosen = jnp.where(slot_number < counts[:, None], unit_order, -1)
    return chosen.reshape(-1).astype(jnp.int32)


def place_ends(result, key, smallest, top_value):
    longest = result.shape.index(max(result.shape))
    spots = []
    for shift in (0, 1):
        where = [jax.random.randint(jax.random.fold_in(key, axis), (), 0, length) for axis, length in enumerate(result.shape)]
        where[longest] = (where[longest] + shift) % result.shape[longest]
        spots.append(tuple(where))
    return result.at[spots[0]].set(smallest).at[spots[1]].set(top_value)


def steps_of(rng, extent, cuts, smallest, largest):
    loudness = 1.0
    for dim, blocks in cuts:
        steps = jax.random.uniform(jax.random.fold_in(jax.random.fold_in(rng, 6), dim), (blocks,), jnp.float32, smallest / len(cuts), largest / len(cuts))
        loudness = loudness * jnp.repeat(jnp.exp(steps), extent[dim] // blocks).reshape((-1,) + (1,) * (len(extent) - 1 - dim))
    return loudness


def bell_draw(own_key, dims, width, bound, pieces=(), kind=jnp.bfloat16):
    level = steps_of(own_key, dims, pieces, -0.22, 0.18) if pieces else 1.0
    values = jax.random.normal(own_key, dims, jnp.float32) * width * level
    return jnp.minimum(jnp.maximum(values, -bound), bound).astype(kind)


def setup_inputs(seed: int = 0) -> dict:
    splits = jax.random.split(jax.random.key(seed), 12)
    out_grad = bell_draw(splits[0], (TOKENS, D), 1.0, 6.0, ((0, 256),))
    gate_pre = bell_draw(splits[1], (TOKENS, FF), 1.0, 6.0, ((0, 8), (1, 32)))
    up_pre = bell_draw(splits[2], (TOKENS, FF), 1.0, 6.0, ((0, 8), (1, 32)))
    gate_codes = place_ends(jax.random.randint(splits[3], (D // 4, FF), 0, 65281), jax.random.fold_in(splits[3], 1), 0, 65280).astype(jnp.int32)
    up_codes = place_ends(jax.random.randint(splits[4], (D // 4, FF), 0, 65281), jax.random.fold_in(splits[4], 1), 0, 65280).astype(jnp.int32)
    down_codes = place_ends(jax.random.randint(splits[5], (FF, D // 4), 0, 65281), jax.random.fold_in(splits[5], 1), 0, 65280).astype(jnp.int32)
    gate_scale = jnp.clip(jnp.exp(math.log(0.006875) - 1.3862944 * jax.random.uniform(splits[6], (D // GROUP, FF), jnp.float32) ** steps_of(splits[6], (D // GROUP, FF), ((1, 32),), -0.2, 0.2)), 0.00171875, 0.006875)
    up_scale = jnp.clip(jnp.exp(math.log(0.006875) - 1.3862944 * jax.random.uniform(splits[7], (D // GROUP, FF), jnp.float32) ** steps_of(splits[7], (D // GROUP, FF), ((1, 32),), -0.2, 0.2)), 0.00171875, 0.006875)
    down_scale = jnp.clip(jnp.exp(math.log(0.0034375) - 1.3862944 * jax.random.uniform(splits[8], (FF // GROUP, D), jnp.float32) ** steps_of(splits[8], (FF // GROUP, D), ((0, 32),), -0.2, 0.2)), 0.000859375, 0.0034375)
    weak_weight = bell_draw(splits[9], (WEAK_SLOTS, D), (FF // 9) ** -0.5, 0.125, ((0, 32),))
    weak_index = draw_weak_index(jax.random.fold_in(splits[11], 71), 0)
    return {"out_grad": out_grad, "gate_pre": gate_pre, "up_pre": up_pre, "gate_codes": gate_codes, "up_codes": up_codes, "down_codes": down_codes, "gate_scale": gate_scale, "up_scale": up_scale, "down_scale": down_scale, "weak_weight": weak_weight, "weak_index": weak_index}


def unpack_levels(packed, unpack_axis):
    nibble_slabs = [(packed // (16 ** nibble)) % 16 for nibble in range(4)]
    return jnp.concatenate(nibble_slabs, axis=unpack_axis).astype(jnp.float32)


def dequant(packed, group_scale, unpack_axis):
    levels = unpack_levels(packed, unpack_axis)
    height, breadth = levels.shape
    groups = group_scale.shape[0]
    grouped = (levels - 7.5).reshape(groups, height // groups, breadth) * group_scale[:, None, :]
    return grouped.reshape(height, breadth)


def reference(out_grad, gate_pre, up_pre, gate_codes, up_codes, down_codes, gate_scale, up_scale, down_scale, weak_weight, weak_index):
    w_gate = dequant(gate_codes, gate_scale, 0).astype(jnp.bfloat16)
    w_up = dequant(up_codes, up_scale, 0).astype(jnp.bfloat16)
    down_plain = dequant(down_codes, down_scale, 1)
    slot_rank = jnp.arange(WEAK_SLOTS, dtype=jnp.int32) // WMAX
    weak_unit = jnp.where(weak_index >= 0, slot_rank * FF_RANK + weak_index, -1).astype(jnp.int32)
    select_mask = jnp.arange(FF, dtype=jnp.int32)[:, None] == weak_unit[None, :]
    select = select_mask.astype(jnp.bfloat16)
    weak_rows = jnp.dot(select, weak_weight, preferred_element_type=jnp.float32)
    is_weak = jnp.any(select_mask, axis=1)
    w_down = jnp.where(is_weak[:, None], weak_rows, down_plain).astype(jnp.bfloat16)
    hidden_grad = jnp.dot(out_grad, w_down.T, preferred_element_type=jnp.float32)
    gate_value = gate_pre.astype(jnp.float32)
    up_value = up_pre.astype(jnp.float32)
    sigmoid_gate = jax.nn.sigmoid(gate_value)
    activated = gate_value * sigmoid_gate
    up_grad = (hidden_grad * activated).astype(jnp.bfloat16)
    gate_grad = (hidden_grad * up_value * sigmoid_gate * (1.0 + gate_value * (1.0 - sigmoid_gate))).astype(jnp.bfloat16)
    in_grad = jnp.dot(gate_grad, w_gate.T, preferred_element_type=jnp.float32) + jnp.dot(up_grad, w_up.T, preferred_element_type=jnp.float32)
    hidden = (activated * up_value).astype(jnp.bfloat16)
    hidden_weak = jnp.dot(hidden, select, preferred_element_type=jnp.float32).astype(jnp.bfloat16)
    weak_grad = jnp.dot(hidden_weak.T, out_grad, preferred_element_type=jnp.float32) * (TOKENS ** -0.5)
    return in_grad.astype(jnp.bfloat16), weak_grad
```

```python
import jax
import jax.numpy as jnp
from jax import lax
from jax.sharding import PartitionSpec as P


X_SIZE, Z_SIZE = 4, 8
X_GROUPS = [[x * Z_SIZE + z for x in range(X_SIZE)] for z in range(Z_SIZE)]
Z_GROUPS = [[x * Z_SIZE + z for z in range(Z_SIZE)] for x in range(X_SIZE)]


def unpack_levels(packed, unpack_axis):
    nibble_slabs = [packed // 16**nibble % 16 for nibble in range(4)]
    return jnp.concatenate(nibble_slabs, axis=unpack_axis).astype(jnp.float32)


def dequant(packed, group_scale, unpack_axis):
    levels = unpack_levels(packed, unpack_axis)
    height, breadth = levels.shape
    groups = group_scale.shape[0]
    grouped = (levels - 7.5).reshape(groups, height // groups, breadth) * group_scale[:, None, :]
    return grouped.reshape(height, breadth)


def contract_last(left_rows, right_rows):
    return lax.dot_general(
        left_rows, right_rows, (((1,), (1,)), ((), ())), preferred_element_type=jnp.float32
    )


def per_device(
    out_grad,
    gate_pre,
    up_pre,
    gate_codes,
    up_codes,
    down_codes,
    gate_scale,
    up_scale,
    down_scale,
    weak_weight,
    weak_index,
):
    w_gate = dequant(gate_codes, gate_scale, 0).astype(jnp.bfloat16)
    w_up = dequant(up_codes, up_scale, 0).astype(jnp.bfloat16)
    down_plain = dequant(down_codes, down_scale, 1)
    unit_count = down_plain.shape[0]
    slot_count = weak_index.shape[0]
    select_mask = (
        lax.broadcasted_iota(jnp.int32, (unit_count, slot_count), 0) == weak_index[None, :]
    )
    select = select_mask.astype(jnp.bfloat16)
    weak_rows = jnp.dot(select, weak_weight, preferred_element_type=jnp.float32)
    is_weak = jnp.any(select_mask, axis=1)
    w_down = jnp.where(is_weak[:, None], weak_rows, down_plain).astype(jnp.bfloat16)
    gate_value = gate_pre.astype(jnp.float32)
    up_value = up_pre.astype(jnp.float32)
    sigmoid_gate = jax.nn.sigmoid(gate_value)
    activated = gate_value * sigmoid_gate
    hidden = (activated * up_value).astype(jnp.bfloat16)
    hidden_weak = jnp.dot(hidden, select, preferred_element_type=jnp.float32).astype(jnp.bfloat16)
    group_tokens = gate_pre.shape[0]
    model_width = out_grad.shape[1]
    arrived = lax.all_gather(out_grad, "tensor", axis=0, tiled=True)
    hidden_grad = contract_last(arrived, w_down)
    up_grad = (hidden_grad * gate_value * sigmoid_gate).astype(jnp.bfloat16)
    gate_grad = (
        hidden_grad * up_value * sigmoid_gate * (1.0 + gate_value * (1.0 - sigmoid_gate))
    ).astype(jnp.bfloat16)
    both_grads = jnp.concatenate([gate_grad, up_grad], axis=1)
    weak_acc = lax.dot_general(
        hidden_weak, arrived, (((0,), (0,)), ((), ())), preferred_element_type=jnp.float32
    )
    dual_grads, weak_acc = (both_grads, weak_acc)
    w_both = jnp.concatenate([w_gate, w_up], axis=1)
    partial = contract_last(dual_grads, w_both).astype(jnp.bfloat16)
    over_x = lax.all_to_all(partial, "tensor", 0, 0, tiled=True, axis_index_groups=X_GROUPS)
    over_x = over_x.reshape(X_SIZE, -1, model_width).astype(jnp.float32).sum(0).astype(jnp.bfloat16)
    over_z = lax.all_to_all(over_x, "tensor", 0, 0, tiled=True, axis_index_groups=Z_GROUPS)
    summed = over_z.reshape(Z_SIZE, -1, model_width).astype(jnp.float32).sum(0).astype(jnp.bfloat16)
    factor = (group_tokens * lax.axis_size("dp")) ** (-0.5)
    weak_sum = lax.psum_scatter(
        weak_acc.astype(jnp.bfloat16), "dp", scatter_dimension=1, tiled=True
    )
    weak_grad = weak_sum.astype(jnp.float32) * factor
    return (summed, weak_grad)


def solution(mesh):
    in_specs = (
        P(("dp", "tensor"), None),
        P("dp", "tensor"),
        P("dp", "tensor"),
        P(None, "tensor"),
        P(None, "tensor"),
        P("tensor", None),
        P(None, "tensor"),
        P(None, "tensor"),
        P("tensor", None),
        P("tensor", None),
        P("tensor"),
    )
    out_specs = (P(("dp", "tensor"), None), P("tensor", "dp"))
    return jax.shard_map(
        per_device, mesh=mesh, in_specs=in_specs, out_specs=out_specs, check_vma=False
    )
```

```python
import functools

import jax
import jax.numpy as jnp
from jax import lax
from jax.experimental import pallas as pl
from jax.experimental.pallas import tpu as pltpu
from jax.sharding import PartitionSpec as P

X, Z = 4, 8
ORDER = [0, 1, 7, 2, 6, 3, 5, 4]
RINGS = [slice(0, 3), slice(3, 5), slice(5, 8)]
PAIRS = [slice(6, 8), slice(4, 6), slice(2, 4), slice(0, 2)]
STEP = 512
GROUP = 128
F32, BF16 = jnp.float32, jnp.bfloat16
VMEM_LIMIT = 20 * 2**20


def shift(block, dx, dz=0):
    pairs = [(x * Z + z, (x + dx) % X * Z + (z + dz) % Z) for x in range(X) for z in range(Z)]
    return lax.ppermute(block, "tensor", pairs)


def after(value, *others):
    any_ = pl.BlockSpec(memory_space=pl.ANY)
    return pl.pallas_call(
        lambda *refs: None,
        in_specs=[any_] * (1 + len(others)),
        out_specs=any_,
        out_shape=jax.ShapeDtypeStruct(value.shape, value.dtype),
        input_output_aliases={0: 0},
        compiler_params=pltpu.CompilerParams(vmem_limit_bytes=2**20),
        name="after",
    )(value, *others)


def nt_dot(left_rows, right_rows):
    return lax.dot_general(
        left_rows, right_rows, (((1,), (1,)), ((), ())), preferred_element_type=F32
    )


def level(codes, nibble):
    return (lax.shift_right_logical(codes, 4 * nibble) & 15).astype(F32) - 7.5


def whole(array):
    return pl.BlockSpec(array.shape, lambda _: (0, 0))


def unpack_kernel(codes, scale, _, out):
    i, steps = pl.program_id(0), pl.num_programs(0)
    for nibble in range(4):
        out[nibble] = (level(codes[...], nibble) * scale[pl.ds(nibble * steps + i, 1), :]).astype(BF16)


def unpack_weights(codes, scale, earlier):
    depth, units = codes.shape
    out = pl.pallas_call(
        unpack_kernel,
        grid=(depth // GROUP,),
        in_specs=[
            pl.BlockSpec((GROUP, units), lambda i: (i, 0)),
            pl.BlockSpec(scale.shape, lambda i: (0, 0)),
            pl.BlockSpec(memory_space=pl.ANY),
        ],
        out_specs=pl.BlockSpec((4, GROUP, units), lambda i: (0, i, 0)),
        out_shape=jax.ShapeDtypeStruct((4, depth, units), BF16),
        cost_estimate=pl.CostEstimate(flops=0, bytes_accessed=6 * 2**20, transcendentals=0),
        compiler_params=pltpu.CompilerParams(vmem_limit_bytes=VMEM_LIMIT),
        name="unpack_weights",
    )(codes, scale, earlier)
    return out.reshape(4 * depth, units)


def down_kernel(codes, scale, weak_weight, weak_index, out):
    i = pl.program_id(0)
    width = codes.shape[1]
    units, slots = codes.shape[0], weak_index.shape[1]
    unit = lax.broadcasted_iota(jnp.int32, (units, slots), 0) + i * units
    mask = (unit == weak_index[...]).astype(F32)
    is_weak = jnp.max(mask, axis=1, keepdims=True) > 0.0
    select = mask.astype(BF16)
    for nibble in range(4):
        part = slice(nibble * width, (nibble + 1) * width)
        plain = level(codes[...], nibble) * scale[pl.ds(i, 1), part]
        weak = jnp.dot(select, weak_weight[:, part], preferred_element_type=F32)
        out[:, part] = jnp.where(is_weak, weak, plain).astype(BF16)


def down_weights(codes, scale, weak_weight, weak_index):
    units, width = codes.shape
    return pl.pallas_call(
        down_kernel,
        grid=(units // GROUP,),
        in_specs=[
            pl.BlockSpec((GROUP, width), lambda i: (i, 0)),
            whole(scale),
            whole(weak_weight),
            whole(weak_index),
        ],
        out_specs=pl.BlockSpec((GROUP, 4 * width), lambda i: (i, 0)),
        out_shape=jax.ShapeDtypeStruct((units, 4 * width), BF16),
        cost_estimate=pl.CostEstimate(flops=0, bytes_accessed=6 * 2**20, transcendentals=0),
        compiler_params=pltpu.CompilerParams(vmem_limit_bytes=VMEM_LIMIT),
        name="down_weights",
    )(codes, scale, weak_weight, weak_index)


def hidden_kernel(sides, place, w_down, gate_pre, up_pre, weak_index, earlier, *refs):
    count = len(sides) * len(RINGS)
    pieces = refs[:count]
    both, weak, arrived, w_copy, active, slope, hidden, sems = refs[count:]
    x, z = place[0], place[1]
    copies = [pltpu.make_async_copy(w_down, w_copy, sems.at[count])]
    for k, piece in enumerate(pieces):
        ring = RINGS[k % len(RINGS)]
        target = arrived.at[k // len(RINGS), pl.ds(ring.start, ring.stop - ring.start)]
        copies.append(pltpu.make_async_copy(piece, target, sems.at[k]))
    for copy in copies:
        copy.start()
    units = gate_pre.shape[1]
    tokens, rows = active.shape[0], pieces[0].shape[1]
    slots = weak_index.shape[1]
    for k, i in enumerate(sides):
        for p, j in enumerate(ORDER):
            source = (((x + i) % X) * Z + (z + j) % Z) * rows
            source = pl.ds(pl.multiple_of(source, rows), rows)
            target = pl.ds((k * Z + p) * rows, rows)
            gate = gate_pre[source, :].astype(F32)
            up = up_pre[source, :].astype(F32)
            sig = jax.nn.sigmoid(gate)
            active[target, :] = gate * sig
            slope[target, :] = up * sig * (1.0 + gate * (1.0 - sig))
            hidden[target, :] = (gate * sig * up).astype(BF16)
    mask = lax.broadcasted_iota(jnp.int32, (units, slots), 0) == weak_index[...]
    select = mask.astype(F32).astype(BF16)
    picked = lax.dot_general(
        select, hidden[...], (((0,), (1,)), ((), ())), preferred_element_type=F32
    ).astype(BF16)
    for copy in copies:
        copy.wait()
    for u in range(0, units, 256):
        part = pl.ds(u, 256)
        grad = nt_dot(arrived[...].reshape(tokens, -1), w_copy[part, :])
        both[:, part] = (grad * slope[:, part]).astype(BF16)
        both[:, pl.ds(units + u, 256)] = (grad * active[:, part]).astype(BF16)
    width = weak.shape[2]
    for k in range(weak.shape[0]):
        part = arrived[:, :, :, k * width : (k + 1) * width].reshape(tokens, width)
        term = jnp.dot(picked, part, preferred_element_type=F32)
        weak[k] = (term if earlier is None else term + earlier[k]).astype(weak.dtype)


def hidden_grads(sides, place, pieces, w_down, gate_pre, up_pre, weak_index, dp, earlier=None):
    units, model = w_down.shape
    tokens = gate_pre.shape[0] // X * len(sides)
    slots = weak_index.shape[1]
    any_ = pl.BlockSpec(memory_space=pl.ANY)
    vmem = pl.BlockSpec(memory_space=pltpu.VMEM)
    flops = 2 * tokens * units * model
    operands = [w_down, gate_pre, up_pre, weak_index]
    kernel = functools.partial(hidden_kernel, sides)
    if earlier is None:
        kernel = lambda *refs: hidden_kernel(sides, *refs[:5], None, *refs[5:])
    else:
        operands.append(earlier)
    return pl.pallas_call(
        kernel,
        in_specs=[pl.BlockSpec(memory_space=pltpu.SMEM), any_]
        + [vmem] * (len(operands) - 1)
        + [any_] * len(pieces),
        out_specs=[vmem, vmem],
        out_shape=[
            jax.ShapeDtypeStruct((tokens, 2 * units), BF16),
            jax.ShapeDtypeStruct((dp, slots, model // dp), F32 if earlier is None else BF16),
        ],
        scratch_shapes=[
            pltpu.VMEM((len(sides), *out_block(gate_pre), model), BF16),
            pltpu.VMEM((units, model), BF16),
            pltpu.VMEM((tokens, units), F32),
            pltpu.VMEM((tokens, units), F32),
            pltpu.VMEM((tokens, units), BF16),
            pltpu.SemaphoreType.DMA((len(pieces) + 1,)),
        ],
        compiler_params=pltpu.CompilerParams(vmem_limit_bytes=VMEM_LIMIT),
        cost_estimate=pl.CostEstimate(flops=flops, bytes_accessed=12 * 2**20, transcendentals=0),
        name="hidden_grads",
    )(place, *operands, *pieces)


def out_block(gate_pre):
    return Z, gate_pre.shape[0] // (X * Z)


def input_kernel(most, far, gate_weights, up_weights, *refs):
    *pieces, both = refs
    rows, step = pieces[0].shape[1:]
    width = gate_weights.shape[1]
    block = far.shape[0]

    @pl.when(pl.program_id(0) == 0)
    def _():
        both[: 2 * block] = most[: 2 * block]
        both[2 * block : 3 * block] = far[...]
        both[3 * block :] = most[2 * block :]

    term = nt_dot(both[:, :width], gate_weights[...]) + nt_dot(both[:, width:], up_weights[...])
    term = term.astype(BF16).reshape(X, Z, rows, step)
    for k, piece in enumerate(pieces):
        piece[...] = term[k // len(PAIRS), PAIRS[k % len(PAIRS)]]


def input_terms(most, far, gate_weights, up_weights):
    tokens, width = X * far.shape[0], far.shape[1]
    model, units = gate_weights.shape
    rows = tokens // (X * Z)
    shapes = [(pair.stop - pair.start, rows) for pair in PAIRS] * X
    weights = pl.BlockSpec((STEP, units), lambda n: (n, 0))
    return pl.pallas_call(
        input_kernel,
        grid=(model // STEP,),
        in_specs=[whole(most), whole(far), weights, weights],
        scratch_shapes=[pltpu.VMEM((tokens, width), BF16)],
        out_specs=[pl.BlockSpec((*shape, STEP), lambda n: (0, 0, n)) for shape in shapes],
        out_shape=[jax.ShapeDtypeStruct((*shape, model), BF16) for shape in shapes],
        compiler_params=pltpu.CompilerParams(vmem_limit_bytes=VMEM_LIMIT),
        cost_estimate=pl.CostEstimate(
            flops=2 * tokens * width * model, bytes_accessed=13 * 2**20, transcendentals=0
        ),
        name="input_terms",
    )(most, far, gate_weights, up_weights)


def total(*terms):
    return functools.reduce(jnp.add, [t.astype(F32) for t in terms])


def per_device(
    out_grad,
    gate_pre,
    up_pre,
    gate_codes,
    up_codes,
    down_codes,
    gate_scale,
    up_scale,
    down_scale,
    weak_weight,
    weak_index,
):
    rank = lax.axis_index("tensor").astype(jnp.int32)
    place = jnp.stack([rank // Z, rank % Z])
    dp = lax.axis_size("dp")
    weak_index = weak_index.reshape(1, -1)

    mine = out_grad[None]
    up, down = shift(mine, 0, 1), shift(mine, 0, -1)
    blocks = {0: mine, 7: up, 1: down}

    def over_x(ring):
        block = jnp.concatenate([blocks[j] for j in ORDER[ring]])
        return [block, shift(block, -1), None, shift(block, 1)]

    w_down = down_weights(down_codes, down_scale, weak_weight, weak_index)
    up = after(up, w_down)
    rings = [over_x(RINGS[0])]
    up, down = shift(up, 0, 1), shift(down, 0, -1)
    blocks |= {6: up, 2: down}
    rings.append(over_x(RINGS[1]))
    w_gate = unpack_weights(gate_codes, gate_scale, down)
    up, down = shift(up, 0, 1), shift(down, 0, -1)
    blocks |= {5: up, 3: down}
    up = after(up, w_gate, rings[0][1], rings[0][3])
    blocks |= {4: shift(up, 0, 1)}
    rings.append(over_x(RINGS[2]))
    rings[0][2] = shift(rings[0][3], 1)
    rings[1][2] = shift(rings[1][3], 1)
    w_up = unpack_weights(up_codes, up_scale, rings[0][2])
    rings[2][2] = shift(after(rings[2][1], w_up), -1)
    near_sides = [0, 1, 3]
    pieces = [ring[i] for i in near_sides for ring in rings]
    saved = (w_down, gate_pre, up_pre, weak_index, dp)
    most, weak = hidden_grads(near_sides, place, pieces, *saved)
    pieces = [ring[2] for ring in rings]
    far, weak = hidden_grads([2], place, pieces, *saved, weak)
    terms = input_terms(most, far, w_gate, w_up)

    def side(i, k):
        return terms[i * len(PAIRS) + k]

    def summed(k, earlier=()):
        order = lambda term: after(term, *earlier) if earlier else term
        relay_up, relay_down = shift(order(side(2, k)), 1), shift(order(side(2, k + 1)), -1)
        plain_down, plain_up = shift(order(side(3, k)), -1), shift(order(side(1, k + 1)), 1)
        near_up = total(side(1, k), relay_up).astype(BF16)
        near_down = total(side(3, k + 1), relay_down).astype(BF16)
        first = total(side(0, k), shift(near_up, 1), plain_down)
        second = total(side(0, k + 1), shift(near_down, -1), plain_up)
        term = {j: first[p] for p, j in enumerate(ORDER[PAIRS[k]])}
        term |= {j: second[p] for p, j in enumerate(ORDER[PAIRS[k + 1]])}
        return term, near_up, near_down, plain_up, plain_down

    term, near_up, near_down, plain_up, plain_down = summed(0)
    up, down = term[4].astype(BF16), term[5].astype(BF16)
    up, down = shift(up, 0, 1), shift(down, 0, -1)
    up, down = total(term[3], up).astype(BF16), total(term[6], down).astype(BF16)
    up, down = shift(up, 0, 1), shift(down, 0, -1)
    weak = lax.all_to_all(after(weak, plain_up, plain_down), "dp", 0, 0, tiled=True)
    term, *_ = summed(2, (near_up, near_down))
    up, down = total(term[2], up).astype(BF16), total(term[7], down).astype(BF16)
    up, down = shift(up, 0, 1), shift(down, 0, -1)
    up = shift(total(term[1], up).astype(BF16), 0, 1)
    in_grad = total(term[0], up, down).astype(BF16)
    factor = (gate_pre.shape[0] * dp) ** (-0.5)
    return in_grad, total(*[weak[k] for k in range(dp)]) * factor


def solution(mesh):
    in_specs = (
        P(("dp", "tensor"), None),
        P("dp", "tensor"),
        P("dp", "tensor"),
        P(None, "tensor"),
        P(None, "tensor"),
        P("tensor", None),
        P(None, "tensor"),
        P(None, "tensor"),
        P("tensor", None),
        P("tensor", None),
        P("tensor"),
    )
    out_specs = (P(("dp", "tensor"), None), P("tensor", "dp"))
    return jax.shard_map(
        per_device, mesh=mesh, in_specs=in_specs, out_specs=out_specs, check_vma=False
    )
```

```python
import functools

import jax
import jax.numpy as jnp
from jax import lax
from jax.experimental import pallas as pl
from jax.experimental.pallas import tpu as pltpu
from jax.sharding import PartitionSpec as P

X, Z = 4, 8
ORDER = [0, 1, 7, 2, 6, 3, 5, 4]
RINGS = [slice(0, 3), slice(3, 5), slice(5, 8)]
PAIRS = [slice(6, 8), slice(4, 6), slice(2, 4), slice(0, 2)]
STEP = 512
GROUP = 128
F32, BF16 = jnp.float32, jnp.bfloat16
VMEM_LIMIT = 20 * 2**20


def shift(block, dx, dz=0):
    pairs = [(x * Z + z, (x + dx) % X * Z + (z + dz) % Z) for x in range(X) for z in range(Z)]
    return lax.ppermute(block, "tensor", pairs)


def after(value, *others):
    any_ = pl.BlockSpec(memory_space=pl.ANY)
    return pl.pallas_call(
        lambda *refs: None,
        in_specs=[any_] * (1 + len(others)),
        out_specs=any_,
        out_shape=jax.ShapeDtypeStruct(value.shape, value.dtype),
        input_output_aliases={0: 0},
        compiler_params=pltpu.CompilerParams(vmem_limit_bytes=2**20),
        name="after",
    )(value, *others)


def nt_dot(left_rows, right_rows):
    return lax.dot_general(
        left_rows, right_rows, (((1,), (1,)), ((), ())), preferred_element_type=F32
    )


def level(codes, nibble):
    return (lax.shift_right_logical(codes, 4 * nibble) & 15).astype(F32) - 7.5


def whole(array):
    return pl.BlockSpec(array.shape, lambda _: (0, 0))


def unpack_kernel(codes, scale, _, out):
    i, steps = pl.program_id(0), pl.num_programs(0)
    for nibble in range(4):
        out[nibble] = (level(codes[...], nibble) * scale[pl.ds(nibble * steps + i, 1), :]).astype(BF16)


def unpack_weights(codes, scale, earlier):
    depth, units = codes.shape
    out = pl.pallas_call(
        unpack_kernel,
        grid=(depth // GROUP,),
        in_specs=[
            pl.BlockSpec((GROUP, units), lambda i: (i, 0)),
            pl.BlockSpec(scale.shape, lambda i: (0, 0)),
            pl.BlockSpec(memory_space=pl.ANY),
        ],
        out_specs=pl.BlockSpec((4, GROUP, units), lambda i: (0, i, 0)),
        out_shape=jax.ShapeDtypeStruct((4, depth, units), BF16),
        cost_estimate=pl.CostEstimate(flops=0, bytes_accessed=6 * 2**20, transcendentals=0),
        compiler_params=pltpu.CompilerParams(vmem_limit_bytes=VMEM_LIMIT),
        name="unpack_weights",
    )(codes, scale, earlier)
    return out.reshape(4 * depth, units)


def down_kernel(codes, scale, weak_weight, weak_index, _, out):
    i = pl.program_id(0)
    width = codes.shape[1]
    units, slots = codes.shape[0], weak_index.shape[1]
    unit = lax.broadcasted_iota(jnp.int32, (units, slots), 0) + i * units
    mask = (unit == weak_index[...]).astype(F32)
    is_weak = jnp.max(mask, axis=1, keepdims=True) > 0.0
    select = mask.astype(BF16)
    for nibble in range(4):
        part = slice(nibble * width, (nibble + 1) * width)
        plain = level(codes[...], nibble) * scale[pl.ds(i, 1), part]
        weak = jnp.dot(select, weak_weight[:, part], preferred_element_type=F32)
        out[:, part] = jnp.where(is_weak, weak, plain).astype(BF16)


def down_weights(codes, scale, weak_weight, weak_index, earlier):
    units, width = codes.shape
    return pl.pallas_call(
        down_kernel,
        grid=(units // GROUP,),
        in_specs=[
            pl.BlockSpec((GROUP, width), lambda i: (i, 0)),
            whole(scale),
            whole(weak_weight),
            whole(weak_index),
            pl.BlockSpec(memory_space=pl.ANY),
        ],
        out_specs=pl.BlockSpec((GROUP, 4 * width), lambda i: (i, 0)),
        out_shape=jax.ShapeDtypeStruct((units, 4 * width), BF16),
        cost_estimate=pl.CostEstimate(flops=0, bytes_accessed=6 * 2**20, transcendentals=0),
        compiler_params=pltpu.CompilerParams(vmem_limit_bytes=VMEM_LIMIT),
        name="down_weights",
    )(codes, scale, weak_weight, weak_index, earlier)


def factor_kernel(place, gate_pre, up_pre, weak_index, _, active, slope, picked, hidden):
    x, z = place[0], place[1]
    tokens, units = gate_pre.shape
    rows = tokens // (X * Z)
    slots = weak_index.shape[1]
    for i in range(X):
        for p, j in enumerate(ORDER):
            source = (((x + i) % X) * Z + (z + j) % Z) * rows
            source = pl.ds(pl.multiple_of(source, rows), rows)
            target = pl.ds((i * Z + p) * rows, rows)
            gate = gate_pre[source, :].astype(F32)
            up = up_pre[source, :].astype(F32)
            sig = jax.nn.sigmoid(gate)
            active[target, :] = gate * sig
            slope[target, :] = up * sig * (1.0 + gate * (1.0 - sig))
            hidden[target, :] = (gate * sig * up).astype(BF16)
    mask = lax.broadcasted_iota(jnp.int32, (units, slots), 0) == weak_index[...]
    select = mask.astype(F32).astype(BF16)
    picked[...] = lax.dot_general(
        select, hidden[...], (((0,), (1,)), ((), ())), preferred_element_type=F32
    ).astype(BF16)


def factors(place, gate_pre, up_pre, weak_index, earlier):
    vmem = pl.BlockSpec(memory_space=pltpu.VMEM)
    smem = pl.BlockSpec(memory_space=pltpu.SMEM)
    tokens, units = gate_pre.shape
    return pl.pallas_call(
        factor_kernel,
        in_specs=[smem, vmem, vmem, vmem, pl.BlockSpec(memory_space=pl.ANY)],
        out_specs=[vmem] * 3,
        out_shape=[
            jax.ShapeDtypeStruct((tokens, units), F32),
            jax.ShapeDtypeStruct((tokens, units), F32),
            jax.ShapeDtypeStruct((weak_index.shape[1], tokens), BF16),
        ],
        scratch_shapes=[pltpu.VMEM((tokens, units), BF16)],
        compiler_params=pltpu.CompilerParams(vmem_limit_bytes=VMEM_LIMIT),
        cost_estimate=pl.CostEstimate(flops=0, bytes_accessed=6 * 2**20, transcendentals=0),
        name="factors",
    )(place, gate_pre, up_pre, weak_index, earlier)


def hidden_kernel(*refs):
    count = X * len(RINGS)
    pieces = refs[:count]
    w_down, active, slope, picked, near, far, weak, arrived, sems = refs[count:]
    copies = []
    for k, piece in enumerate(pieces):
        ring = RINGS[k % len(RINGS)]
        target = arrived.at[k // len(RINGS), pl.ds(ring.start, ring.stop - ring.start)]
        copies.append(pltpu.make_async_copy(piece, target, sems.at[k]))
    for copy in copies:
        copy.start()
    for copy in copies:
        copy.wait()
    tokens, units = active.shape
    for u in range(0, units, 256):
        grad = nt_dot(arrived[...].reshape(tokens, -1), w_down[pl.ds(u, 256), :])
        for column, factor in ((u, slope), (units + u, active)):
            term = (grad * factor[:, pl.ds(u, 256)]).astype(BF16).reshape(X, 2, -1, 256)
            near[:, :, pl.ds(column, 256)] = term[:, 0]
            far[:, :, pl.ds(column, 256)] = term[:, 1]
    width = weak.shape[2]
    for k in range(weak.shape[0]):
        part = arrived[:, :, :, k * width : (k + 1) * width].reshape(tokens, width)
        weak[k] = jnp.dot(picked[...], part, preferred_element_type=F32).astype(BF16)


def hidden_grads(pieces, w_down, active, slope, picked, dp):
    tokens, units = active.shape
    model = w_down.shape[1]
    any_ = pl.BlockSpec(memory_space=pl.ANY)
    vmem = pl.BlockSpec(memory_space=pltpu.VMEM)
    flops = 2 * tokens * units * model
    return pl.pallas_call(
        hidden_kernel,
        in_specs=[any_] * len(pieces) + [vmem] * 4,
        out_specs=[vmem] * 3,
        out_shape=[jax.ShapeDtypeStruct((X, tokens // (2 * X), 2 * units), BF16)] * 2
        + [
            jax.ShapeDtypeStruct((dp, picked.shape[0], model // dp), BF16),
        ],
        scratch_shapes=[
            pltpu.VMEM((X, Z, tokens // (X * Z), model), BF16),
            pltpu.SemaphoreType.DMA((len(pieces),)),
        ],
        compiler_params=pltpu.CompilerParams(vmem_limit_bytes=VMEM_LIMIT),
        cost_estimate=pl.CostEstimate(flops=flops, bytes_accessed=12 * 2**20, transcendentals=0),
        name="hidden_grads",
    )(*pieces, w_down, active, slope, picked)


def input_kernel(both, gate_weights, up_weights, *pieces):
    rows, step = pieces[0].shape[1:]
    width = gate_weights.shape[1]
    left, right = both[..., :width].reshape(-1, width), both[..., width:].reshape(-1, width)
    term = nt_dot(left, gate_weights[...]) + nt_dot(right, up_weights[...])
    term = term.astype(BF16).reshape(X, 2, -1, rows, step)
    for k, piece in enumerate(pieces):
        piece[...] = term[k // 2, 1 - k % 2]


def input_terms(both, gate_weights, up_weights):
    tokens, width = both.shape[0] * both.shape[1], both.shape[2]
    model, units = gate_weights.shape
    shape = (Z // 4, tokens // (X * Z // 2))
    weights = pl.BlockSpec((STEP, units), lambda n: (n, 0))
    return pl.pallas_call(
        input_kernel,
        grid=(model // STEP,),
        in_specs=[pl.BlockSpec(both.shape, lambda n: (0, 0, 0)), weights, weights],
        out_specs=[pl.BlockSpec((*shape, STEP), lambda n: (0, 0, n))] * (2 * X),
        out_shape=[jax.ShapeDtypeStruct((*shape, model), BF16)] * (2 * X),
        compiler_params=pltpu.CompilerParams(vmem_limit_bytes=VMEM_LIMIT),
        cost_estimate=pl.CostEstimate(
            flops=2 * tokens * width * model, bytes_accessed=11 * 2**20, transcendentals=0
        ),
        name="input_terms",
    )(both, gate_weights, up_weights)


def total(*terms):
    return functools.reduce(jnp.add, [t.astype(F32) for t in terms])


def per_device(
    out_grad,
    gate_pre,
    up_pre,
    gate_codes,
    up_codes,
    down_codes,
    gate_scale,
    up_scale,
    down_scale,
    weak_weight,
    weak_index,
):
    rank = lax.axis_index("tensor").astype(jnp.int32)
    place = jnp.stack([rank // Z, rank % Z])
    dp = lax.axis_size("dp")
    weak_index = weak_index.reshape(1, -1)

    mine = out_grad[None]
    blocks = {0: mine}

    def near(ring):
        return jnp.concatenate([blocks[j] for j in ORDER[ring]])

    def over_x(block):
        return [block, shift(block, -1), None, shift(block, 1)]

    up, down = shift(mine, 0, 1), shift(mine, 0, -1)
    blocks |= {7: up, 1: down}
    block = near(RINGS[0])
    rings = [over_x(block)]
    up, down = shift(after(up, block), 0, 1), shift(down, 0, -1)
    blocks |= {6: up, 2: down}
    block = near(RINGS[1])
    rings.append(over_x(block))
    across = shift(after(down, rings[0][1], rings[0][3]), 0, -2)
    up, down = shift(after(up, block), 0, 1), shift(down, 0, -1)
    blocks |= {5: up, 3: down, 4: across}
    rings.append(over_x(after(near(RINGS[2]), rings[1][1], rings[1][3])))
    rings[0][2] = shift(rings[0][3], 1)
    rings[1][2] = shift(rings[1][3], 1)
    w_down = down_weights(down_codes, down_scale, weak_weight, weak_index, across)
    w_gate = unpack_weights(gate_codes, gate_scale, rings[1][1])
    active, slope, picked = factors(place, gate_pre, up_pre, weak_index, across)
    w_up = unpack_weights(up_codes, up_scale, rings[0][2])
    rings[2][2] = shift(after(rings[2][1], w_up, w_gate), -1)
    pieces = [ring[i] for i in range(X) for ring in rings]
    near, far, weak = hidden_grads(pieces, w_down, active, slope, picked, dp)
    terms = [input_terms(half, w_gate, w_up) for half in (far, near)]

    def side(i, k):
        return terms[k // 2][2 * i + k % 2]

    def summed(k, earlier=()):
        order = lambda term: after(term, *earlier) if earlier else term
        relay_up, relay_down = shift(order(side(2, k)), 1), shift(order(side(2, k + 1)), -1)
        plain_down, plain_up = shift(order(side(3, k)), -1), shift(order(side(1, k + 1)), 1)
        near_up = total(side(1, k), relay_up).astype(BF16)
        near_down = total(side(3, k + 1), relay_down).astype(BF16)
        first = total(side(0, k), shift(near_up, 1), plain_down)
        second = total(side(0, k + 1), shift(near_down, -1), plain_up)
        term = {j: first[p] for p, j in enumerate(ORDER[PAIRS[k]])}
        term |= {j: second[p] for p, j in enumerate(ORDER[PAIRS[k + 1]])}
        return term, near_up, near_down, plain_up, plain_down

    term, near_up, near_down, plain_up, plain_down = summed(0)
    up, down = term[4].astype(BF16), term[5].astype(BF16)
    up, down = shift(up, 0, 1), shift(down, 0, -1)
    up, down = total(term[3], up).astype(BF16), total(term[6], down).astype(BF16)
    up, down = shift(up, 0, 1), shift(down, 0, -1)
    weak = lax.all_to_all(after(weak, near_up, near_down), "dp", 0, 0, tiled=True)
    term, *_ = summed(2, (plain_up, plain_down))
    up, down = total(term[2], up).astype(BF16), total(term[7], down).astype(BF16)
    up, down = shift(up, 0, 1), shift(down, 0, -1)
    up = shift(total(term[1], up).astype(BF16), 0, 1)
    in_grad = total(term[0], up, down).astype(BF16)
    factor = (gate_pre.shape[0] * dp) ** (-0.5)
    return in_grad, total(*[weak[k] for k in range(dp)]) * factor


def solution(mesh):
    in_specs = (
        P(("dp", "tensor"), None),
        P("dp", "tensor"),
        P("dp", "tensor"),
        P(None, "tensor"),
        P(None, "tensor"),
        P("tensor", None),
        P(None, "tensor"),
        P(None, "tensor"),
        P("tensor", None),
        P("tensor", None),
        P("tensor"),
    )
    out_specs = (P(("dp", "tensor"), None), P("tensor", "dp"))
    return jax.shard_map(
        per_device, mesh=mesh, in_specs=in_specs, out_specs=out_specs, check_vma=False
    )
```

```python
import functools

import jax
import jax.numpy as jnp
from jax import lax
from jax.experimental import pallas as pl
from jax.experimental.pallas import tpu as pltpu
from jax.sharding import PartitionSpec as P

X, Z = 4, 8
ORDER = [0, 1, 7, 2, 6, 3, 5, 4]
RINGS = [slice(0, 3), slice(3, 5), slice(5, 8)]
PAIRS = [slice(6, 8), slice(4, 6), slice(2, 4), slice(0, 2)]
STEP = 512
HALF = Z // 2
QUARTERS = [(0, 0), (1, 0), (3, 0), (2, 0), (0, 1), (1, 1), (2, 1), (3, 1)]
EARLY = 3
GROUP = 128
F32, BF16 = jnp.float32, jnp.bfloat16
VMEM_LIMIT = 20 * 2**20


def shift(block, dx, dz=0):
    pairs = [(x * Z + z, (x + dx) % X * Z + (z + dz) % Z) for x in range(X) for z in range(Z)]
    return lax.ppermute(block, "tensor", pairs)


def after(value, *others):
    any_ = pl.BlockSpec(memory_space=pl.ANY)
    return pl.pallas_call(
        lambda *refs: None,
        in_specs=[any_] * (1 + len(others)),
        out_specs=any_,
        out_shape=jax.ShapeDtypeStruct(value.shape, value.dtype),
        input_output_aliases={0: 0},
        compiler_params=pltpu.CompilerParams(vmem_limit_bytes=2**20),
        name="after",
    )(value, *others)


def nt_dot(left_rows, right_rows):
    return lax.dot_general(
        left_rows, right_rows, (((1,), (1,)), ((), ())), preferred_element_type=F32
    )


def level(codes, nibble):
    return (lax.shift_right_logical(codes, 4 * nibble) & 15).astype(F32) - 7.5


def whole(array):
    return pl.BlockSpec(array.shape, lambda _: (0, 0))


def unpack_kernel(codes, scale, _, out):
    i, steps = pl.program_id(0), pl.num_programs(0)
    for nibble in range(4):
        out[nibble] = (level(codes[...], nibble) * scale[pl.ds(nibble * steps + i, 1), :]).astype(BF16)


def unpack_weights(codes, scale, earlier):
    depth, units = codes.shape
    out = pl.pallas_call(
        unpack_kernel,
        grid=(depth // GROUP,),
        in_specs=[
            pl.BlockSpec((GROUP, units), lambda i: (i, 0)),
            pl.BlockSpec(scale.shape, lambda i: (0, 0)),
            pl.BlockSpec(memory_space=pl.ANY),
        ],
        out_specs=pl.BlockSpec((4, GROUP, units), lambda i: (0, i, 0)),
        out_shape=jax.ShapeDtypeStruct((4, depth, units), BF16),
        cost_estimate=pl.CostEstimate(flops=0, bytes_accessed=6 * 2**20, transcendentals=0),
        compiler_params=pltpu.CompilerParams(vmem_limit_bytes=VMEM_LIMIT),
        name="unpack_weights",
    )(codes, scale, earlier)
    return out.reshape(4 * depth, units)


def down_kernel(codes, scale, weak_weight, weak_index, _, out):
    i = pl.program_id(0)
    width = codes.shape[1]
    units, slots = codes.shape[0], weak_index.shape[1]
    unit = lax.broadcasted_iota(jnp.int32, (units, slots), 0) + i * units
    mask = (unit == weak_index[...]).astype(F32)
    is_weak = jnp.max(mask, axis=1, keepdims=True) > 0.0
    select = mask.astype(BF16)
    for nibble in range(4):
        part = slice(nibble * width, (nibble + 1) * width)
        plain = level(codes[...], nibble) * scale[pl.ds(i, 1), part]
        weak = jnp.dot(select, weak_weight[:, part], preferred_element_type=F32)
        out[:, part] = jnp.where(is_weak, weak, plain).astype(BF16)


def down_weights(codes, scale, weak_weight, weak_index, earlier):
    units, width = codes.shape
    return pl.pallas_call(
        down_kernel,
        grid=(units // GROUP,),
        in_specs=[
            pl.BlockSpec((GROUP, width), lambda i: (i, 0)),
            whole(scale),
            whole(weak_weight),
            whole(weak_index),
            pl.BlockSpec(memory_space=pl.ANY),
        ],
        out_specs=pl.BlockSpec((GROUP, 4 * width), lambda i: (i, 0)),
        out_shape=jax.ShapeDtypeStruct((units, 4 * width), BF16),
        cost_estimate=pl.CostEstimate(flops=0, bytes_accessed=6 * 2**20, transcendentals=0),
        compiler_params=pltpu.CompilerParams(vmem_limit_bytes=VMEM_LIMIT),
        name="down_weights",
    )(codes, scale, weak_weight, weak_index, earlier)


def factor_kernel(place, gate_pre, up_pre, weak_index, _, active, slope, early, late, hidden):
    x, z = place[0], place[1]
    tokens, units = gate_pre.shape
    rows = tokens // (X * Z)
    slots = weak_index.shape[1]
    for i in range(X):
        for p, j in enumerate(ORDER):
            source = (((x + i) % X) * Z + (z + j) % Z) * rows
            source = pl.ds(pl.multiple_of(source, rows), rows)
            target = QUARTERS.index((i, p // HALF)) * HALF + p % HALF
            target = pl.ds(target * rows, rows)
            gate = gate_pre[source, :].astype(F32)
            up = up_pre[source, :].astype(F32)
            sig = jax.nn.sigmoid(gate)
            active[target, :] = gate * sig
            slope[target, :] = up * sig * (1.0 + gate * (1.0 - sig))
            hidden[target, :] = (gate * sig * up).astype(BF16)
    mask = lax.broadcasted_iota(jnp.int32, (units, slots), 0) == weak_index[...]
    select = mask.astype(F32).astype(BF16)
    cut = early.shape[1]
    for picked, part in ((early, hidden[:cut]), (late, hidden[cut:])):
        picked[...] = lax.dot_general(
            select, part, (((0,), (1,)), ((), ())), preferred_element_type=F32
        ).astype(BF16)


def factors(place, gate_pre, up_pre, weak_index, earlier):
    vmem = pl.BlockSpec(memory_space=pltpu.VMEM)
    smem = pl.BlockSpec(memory_space=pltpu.SMEM)
    tokens, units = gate_pre.shape
    return pl.pallas_call(
        factor_kernel,
        in_specs=[smem, vmem, vmem, vmem, pl.BlockSpec(memory_space=pl.ANY)],
        out_specs=[vmem] * 4,
        out_shape=[
            jax.ShapeDtypeStruct((tokens, units), F32),
            jax.ShapeDtypeStruct((tokens, units), F32),
            jax.ShapeDtypeStruct((weak_index.shape[1], tokens // len(QUARTERS) * EARLY), BF16),
            jax.ShapeDtypeStruct((weak_index.shape[1], tokens // len(QUARTERS) * (len(QUARTERS) - EARLY)), BF16),
        ],
        scratch_shapes=[pltpu.VMEM((tokens, units), BF16)],
        compiler_params=pltpu.CompilerParams(vmem_limit_bytes=VMEM_LIMIT),
        cost_estimate=pl.CostEstimate(flops=0, bytes_accessed=6 * 2**20, transcendentals=0),
        name="factors",
    )(place, gate_pre, up_pre, weak_index, earlier)


def parts_of(quarters):
    parts = []
    for n, (i, half) in enumerate(quarters):
        for k, ring in enumerate(RINGS):
            first, last = max(ring.start, half * HALF), min(ring.stop, (half + 1) * HALF)
            if first < last:
                parts.append((n, i, k, first - ring.start, first - half * HALF, last - first))
    return parts


def hidden_kernel(start, parts, *refs):
    pieces = refs[: len(parts)]
    w_down, active, slope, picked, earlier, both, weak, arrived, sems = refs[len(parts) :]
    copies = []
    for k, (n, _, _, source, target, count) in enumerate(parts):
        source, target = pl.ds(source, count), pl.ds(target, count)
        copies.append(
            pltpu.make_async_copy(pieces[k].at[source], arrived.at[n, target], sems.at[k])
        )
    for copy in copies:
        copy.start()
    for copy in copies:
        copy.wait()
    units = active.shape[1]
    tokens = both.shape[0]
    mine = pl.ds(start, tokens)
    for u in range(0, units, 256):
        part = pl.ds(u, 256)
        grad = nt_dot(arrived[...].reshape(tokens, -1), w_down[part, :])
        both[:, part] = (grad * slope[mine, part]).astype(BF16)
        both[:, pl.ds(units + u, 256)] = (grad * active[mine, part]).astype(BF16)
    width = weak.shape[2]
    for k in range(weak.shape[0]):
        part = arrived[:, :, :, k * width : (k + 1) * width].reshape(tokens, width)
        term = jnp.dot(picked[...], part, preferred_element_type=F32)
        weak[k] = (term if earlier is None else term + earlier[k]).astype(weak.dtype)


def hidden_grads(first, last, rings, w_down, active, slope, picked, dp, *earlier):
    units = active.shape[1]
    quarter = active.shape[0] // len(QUARTERS)
    tokens = (last - first) * quarter
    model = w_down.shape[1]
    parts = parts_of(QUARTERS[first:last])
    pieces = [rings[k][i] for _, i, k, *_ in parts]
    any_ = pl.BlockSpec(memory_space=pl.ANY)
    vmem = pl.BlockSpec(memory_space=pltpu.VMEM)
    flops = 2 * tokens * units * model
    kernel = functools.partial(hidden_kernel, first * quarter, parts)
    if not earlier:
        count = len(pieces) + 4
        kernel = lambda *refs: hidden_kernel(
            first * quarter, parts, *refs[:count], None, *refs[count:]
        )
    return pl.pallas_call(
        kernel,
        in_specs=[any_] * len(pieces) + [vmem] * 4 + [vmem] * len(earlier),
        out_specs=[vmem, vmem],
        out_shape=[
            jax.ShapeDtypeStruct((tokens, 2 * units), BF16),
            jax.ShapeDtypeStruct(
                (dp, picked.shape[0], model // dp), BF16 if earlier else F32
            ),
        ],
        scratch_shapes=[
            pltpu.VMEM((last - first, HALF, quarter // HALF, model), BF16),
            pltpu.SemaphoreType.DMA((len(pieces),)),
        ],
        compiler_params=pltpu.CompilerParams(vmem_limit_bytes=VMEM_LIMIT),
        cost_estimate=pl.CostEstimate(flops=flops, bytes_accessed=8 * 2**20, transcendentals=0),
        name="hidden_grads",
    )(*pieces, w_down, active, slope, picked, *earlier)


def input_kernel(sides, far, early, late, gate_weights, up_weights, _, *refs):
    *pieces, both = refs
    rows, step = pieces[0].shape[1:]
    width = gate_weights.shape[1]
    cut, quarter = early.shape[0], both.shape[0] // X

    @pl.when(pl.program_id(0) == 0)
    def _():
        if far:
            both[...] = late[quarter:]
        else:
            both[:cut] = early[...]
            both[cut:] = late[:quarter]

    term = nt_dot(both[:, :width], gate_weights[...]) + nt_dot(both[:, width:], up_weights[...])
    term = term.astype(BF16).reshape(X, 2, -1, rows, step)
    for k, piece in enumerate(pieces):
        piece[...] = term[sides.index(k // 2), 1 - k % 2]


def input_terms(far, early, late, gate_weights, up_weights, earlier):
    tokens, width = (early.shape[0] + late.shape[0]) // 2, early.shape[1]
    model, units = gate_weights.shape
    shape = (Z // 4, tokens // (X * Z // 2))
    sides = [i for i, half in QUARTERS if half == far]
    weights = pl.BlockSpec((STEP, units), lambda n: (n, 0))
    return pl.pallas_call(
        functools.partial(input_kernel, sides, far),
        grid=(model // STEP,),
        in_specs=[whole(early), whole(late), weights, weights, pl.BlockSpec(memory_space=pl.ANY)],
        out_specs=[pl.BlockSpec((*shape, STEP), lambda n: (0, 0, n))] * (2 * X),
        out_shape=[jax.ShapeDtypeStruct((*shape, model), BF16)] * (2 * X),
        scratch_shapes=[pltpu.VMEM((tokens, width), BF16)],
        compiler_params=pltpu.CompilerParams(vmem_limit_bytes=VMEM_LIMIT),
        cost_estimate=pl.CostEstimate(
            flops=2 * tokens * width * model, bytes_accessed=11 * 2**20, transcendentals=0
        ),
        name="input_terms",
    )(early, late, gate_weights, up_weights, earlier)


def total(*terms):
    return functools.reduce(jnp.add, [t.astype(F32) for t in terms])


def per_device(
    out_grad,
    gate_pre,
    up_pre,
    gate_codes,
    up_codes,
    down_codes,
    gate_scale,
    up_scale,
    down_scale,
    weak_weight,
    weak_index,
):
    rank = lax.axis_index("tensor").astype(jnp.int32)
    place = jnp.stack([rank // Z, rank % Z])
    dp = lax.axis_size("dp")
    weak_index = weak_index.reshape(1, -1)

    mine = out_grad[None]
    blocks = {0: mine}

    def near(ring):
        return jnp.concatenate([blocks[j] for j in ORDER[ring]])

    def over_x(block):
        return [block, shift(block, -1), None, shift(block, 1)]

    up, down = shift(mine, 0, 1), shift(mine, 0, -1)
    blocks |= {7: up, 1: down}
    block = near(RINGS[0])
    rings = [over_x(block)]
    up, down = shift(after(up, block), 0, 1), shift(down, 0, -1)
    blocks |= {6: up, 2: down}
    block = near(RINGS[1])
    rings.append(over_x(block))
    across = shift(after(down, rings[0][1], rings[0][3]), 0, -2)
    up, down = shift(after(up, block), 0, 1), shift(down, 0, -1)
    blocks |= {5: up, 3: down, 4: across}
    rings.append(over_x(after(near(RINGS[2]), rings[1][1], rings[1][3])))
    rings[0][2] = shift(rings[0][3], 1)
    rings[1][2] = shift(rings[1][3], 1)
    w_down = down_weights(down_codes, down_scale, weak_weight, weak_index, rings[1][1])
    w_gate = unpack_weights(gate_codes, gate_scale, rings[1][1])
    active, slope, *picked = factors(place, gate_pre, up_pre, weak_index, rings[0][1])
    w_up = unpack_weights(up_codes, up_scale, rings[0][2])
    rings[2][2] = shift(after(rings[2][1], w_up, w_gate, w_down, active), -1)
    saved = (rings, w_down, active, slope)
    early, weak = hidden_grads(0, EARLY, *saved, picked[0], dp)
    late, weak = hidden_grads(EARLY, len(QUARTERS), *saved, picked[1], dp, weak)
    terms = [input_terms(1, early, late, w_gate, w_up, late)]
    terms.append(input_terms(0, early, late, w_gate, w_up, terms[0][0]))

    def side(i, k):
        return terms[k // 2][2 * i + k % 2]

    def summed(k, earlier=()):
        order = lambda term: after(term, *earlier) if earlier else term
        relay_up, relay_down = shift(order(side(2, k)), 1), shift(order(side(2, k + 1)), -1)
        plain_down, plain_up = shift(order(side(3, k)), -1), shift(order(side(1, k + 1)), 1)
        near_up = total(side(1, k), relay_up).astype(BF16)
        near_down = total(side(3, k + 1), relay_down).astype(BF16)
        first = total(side(0, k), shift(near_up, 1), plain_down)
        second = total(side(0, k + 1), shift(near_down, -1), plain_up)
        term = {j: first[p] for p, j in enumerate(ORDER[PAIRS[k]])}
        term |= {j: second[p] for p, j in enumerate(ORDER[PAIRS[k + 1]])}
        return term, near_up, near_down, plain_up, plain_down

    term, near_up, near_down, plain_up, plain_down = summed(0)
    up, down = term[4].astype(BF16), term[5].astype(BF16)
    up, down = shift(up, 0, 1), shift(down, 0, -1)
    up, down = total(term[3], up).astype(BF16), total(term[6], down).astype(BF16)
    up, down = shift(up, 0, 1), shift(down, 0, -1)
    weak = lax.all_to_all(after(weak, near_up, near_down), "dp", 0, 0, tiled=True)
    term, *_ = summed(2, (plain_up, plain_down))
    up, down = total(term[2], up).astype(BF16), total(term[7], down).astype(BF16)
    up, down = shift(up, 0, 1), shift(down, 0, -1)
    up = shift(total(term[1], up).astype(BF16), 0, 1)
    in_grad = total(term[0], up, down).astype(BF16)
    factor = (gate_pre.shape[0] * dp) ** (-0.5)
    return in_grad, total(*[weak[k] for k in range(dp)]) * factor


def solution(mesh):
    in_specs = (
        P(("dp", "tensor"), None),
        P("dp", "tensor"),
        P("dp", "tensor"),
        P(None, "tensor"),
        P(None, "tensor"),
        P("tensor", None),
        P(None, "tensor"),
        P(None, "tensor"),
        P("tensor", None),
        P("tensor", None),
        P("tensor"),
    )
    out_specs = (P(("dp", "tensor"), None), P("tensor", "dp"))
    return jax.shard_map(
        per_device, mesh=mesh, in_specs=in_specs, out_specs=out_specs, check_vma=False
    )
```

```python
import functools

import jax
import jax.numpy as jnp
from jax import lax
from jax.experimental import pallas as pl
from jax.experimental.pallas import tpu as pltpu
from jax.sharding import PartitionSpec as P

X, Z = 4, 8
ORDER = [0, 1, 7, 2, 6, 3, 5, 4]
RINGS = [slice(0, 3), slice(3, 5), slice(5, 8)]
PAIRS = [slice(6, 8), slice(4, 6), slice(2, 4), slice(0, 2)]
STEP = 1024
HALF = Z // 2
QUARTERS = [(0, 0), (1, 0), (3, 0), (2, 0), (0, 1), (1, 1), (2, 1), (3, 1)]
EARLY = 3
GROUP = 128
F32, BF16 = jnp.float32, jnp.bfloat16
VMEM_LIMIT = 20 * 2**20


def shift(block, dx, dz=0):
    pairs = [(x * Z + z, (x + dx) % X * Z + (z + dz) % Z) for x in range(X) for z in range(Z)]
    return lax.ppermute(block, "tensor", pairs)


def after(value, *others):
    any_ = pl.BlockSpec(memory_space=pl.ANY)
    return pl.pallas_call(
        lambda *refs: None,
        in_specs=[any_] * (1 + len(others)),
        out_specs=any_,
        out_shape=jax.ShapeDtypeStruct(value.shape, value.dtype),
        input_output_aliases={0: 0},
        compiler_params=pltpu.CompilerParams(vmem_limit_bytes=2**20),
        name="after",
    )(value, *others)


def nt_dot(left_rows, right_rows):
    return lax.dot_general(
        left_rows, right_rows, (((1,), (1,)), ((), ())), preferred_element_type=F32
    )


def level(codes, nibble):
    return (lax.shift_right_logical(codes, 4 * nibble) & 15).astype(F32) - 7.5


def whole(array):
    return pl.BlockSpec(array.shape, lambda _: (0, 0))


def unpack_kernel(codes, scale, _, out):
    i, steps = pl.program_id(0), pl.num_programs(0)
    for nibble in range(4):
        out[nibble] = (level(codes[...], nibble) * scale[pl.ds(nibble * steps + i, 1), :]).astype(BF16)


def unpack_weights(codes, scale, earlier):
    depth, units = codes.shape
    out = pl.pallas_call(
        unpack_kernel,
        grid=(depth // GROUP,),
        in_specs=[
            pl.BlockSpec((GROUP, units), lambda i: (i, 0)),
            pl.BlockSpec(scale.shape, lambda i: (0, 0)),
            pl.BlockSpec(memory_space=pl.ANY),
        ],
        out_specs=pl.BlockSpec((4, GROUP, units), lambda i: (0, i, 0)),
        out_shape=jax.ShapeDtypeStruct((4, depth, units), BF16),
        cost_estimate=pl.CostEstimate(flops=0, bytes_accessed=6 * 2**20, transcendentals=0),
        compiler_params=pltpu.CompilerParams(vmem_limit_bytes=VMEM_LIMIT),
        name="unpack_weights",
    )(codes, scale, earlier)
    return out.reshape(4 * depth, units)


def down_kernel(codes, scale, weak_weight, weak_index, _, out):
    i = pl.program_id(0)
    width = codes.shape[1]
    units, slots = codes.shape[0], weak_index.shape[1]
    unit = lax.broadcasted_iota(jnp.int32, (units, slots), 0) + i * units
    mask = (unit == weak_index[...]).astype(F32)
    is_weak = jnp.max(mask, axis=1, keepdims=True) > 0.0
    select = mask.astype(BF16)
    for nibble in range(4):
        part = slice(nibble * width, (nibble + 1) * width)
        plain = level(codes[...], nibble) * scale[pl.ds(i, 1), part]
        weak = jnp.dot(select, weak_weight[:, part], preferred_element_type=F32)
        out[:, part] = jnp.where(is_weak, weak, plain).astype(BF16)


def down_weights(codes, scale, weak_weight, weak_index, earlier):
    units, width = codes.shape
    return pl.pallas_call(
        down_kernel,
        grid=(units // GROUP,),
        in_specs=[
            pl.BlockSpec((GROUP, width), lambda i: (i, 0)),
            whole(scale),
            whole(weak_weight),
            whole(weak_index),
            pl.BlockSpec(memory_space=pl.ANY),
        ],
        out_specs=pl.BlockSpec((GROUP, 4 * width), lambda i: (i, 0)),
        out_shape=jax.ShapeDtypeStruct((units, 4 * width), BF16),
        cost_estimate=pl.CostEstimate(flops=0, bytes_accessed=6 * 2**20, transcendentals=0),
        compiler_params=pltpu.CompilerParams(vmem_limit_bytes=VMEM_LIMIT),
        name="down_weights",
    )(codes, scale, weak_weight, weak_index, earlier)


def factor_kernel(place, gate_pre, up_pre, weak_index, _, active, slope, early, late, hidden):
    x, z = place[0], place[1]
    tokens, units = gate_pre.shape
    rows = tokens // (X * Z)
    slots = weak_index.shape[1]
    for i in range(X):
        for p, j in enumerate(ORDER):
            source = (((x + i) % X) * Z + (z + j) % Z) * rows
            source = pl.ds(pl.multiple_of(source, rows), rows)
            target = QUARTERS.index((i, p // HALF)) * HALF + p % HALF
            target = pl.ds(target * rows, rows)
            gate = gate_pre[source, :].astype(F32)
            up = up_pre[source, :].astype(F32)
            sig = jax.nn.sigmoid(gate)
            active[target, :] = gate * sig
            slope[target, :] = up * sig * (1.0 + gate * (1.0 - sig))
            hidden[target, :] = (gate * sig * up).astype(BF16)
    mask = lax.broadcasted_iota(jnp.int32, (units, slots), 0) == weak_index[...]
    select = mask.astype(F32).astype(BF16)
    cut = early.shape[1]
    for picked, part in ((early, hidden[:cut]), (late, hidden[cut:])):
        picked[...] = lax.dot_general(
            select, part, (((0,), (1,)), ((), ())), preferred_element_type=F32
        ).astype(BF16)


def factors(place, gate_pre, up_pre, weak_index, earlier):
    vmem = pl.BlockSpec(memory_space=pltpu.VMEM)
    smem = pl.BlockSpec(memory_space=pltpu.SMEM)
    tokens, units = gate_pre.shape
    return pl.pallas_call(
        factor_kernel,
        in_specs=[smem, vmem, vmem, vmem, pl.BlockSpec(memory_space=pl.ANY)],
        out_specs=[vmem] * 4,
        out_shape=[
            jax.ShapeDtypeStruct((tokens, units), F32),
            jax.ShapeDtypeStruct((tokens, units), F32),
            jax.ShapeDtypeStruct((weak_index.shape[1], tokens // len(QUARTERS) * EARLY), BF16),
            jax.ShapeDtypeStruct((weak_index.shape[1], tokens // len(QUARTERS) * (len(QUARTERS) - EARLY)), BF16),
        ],
        scratch_shapes=[pltpu.VMEM((tokens, units), BF16)],
        compiler_params=pltpu.CompilerParams(vmem_limit_bytes=VMEM_LIMIT),
        cost_estimate=pl.CostEstimate(flops=0, bytes_accessed=6 * 2**20, transcendentals=0),
        name="factors",
    )(place, gate_pre, up_pre, weak_index, earlier)


def parts_of(quarters):
    parts = []
    for n, (i, half) in enumerate(quarters):
        for k, ring in enumerate(RINGS):
            first, last = max(ring.start, half * HALF), min(ring.stop, (half + 1) * HALF)
            if first < last:
                parts.append((n, i, k, first - ring.start, first - half * HALF, last - first))
    return parts


def hidden_kernel(start, parts, *refs):
    pieces = refs[: len(parts)]
    w_down, active, slope, picked, earlier, both, weak, arrived, sems = refs[len(parts) :]
    copies = []
    for k, (n, _, _, source, target, count) in enumerate(parts):
        source, target = pl.ds(source, count), pl.ds(target, count)
        copies.append(
            pltpu.make_async_copy(pieces[k].at[source], arrived.at[n, target], sems.at[k])
        )
    for copy in copies:
        copy.start()
    for copy in copies:
        copy.wait()
    units = active.shape[1]
    tokens = both.shape[0]
    mine = pl.ds(start, tokens)
    for u in range(0, units, 512):
        part = pl.ds(u, 512)
        grad = nt_dot(arrived[...].reshape(tokens, -1), w_down[part, :])
        both[:, part] = (grad * slope[mine, part]).astype(BF16)
        both[:, pl.ds(units + u, 512)] = (grad * active[mine, part]).astype(BF16)
    width = weak.shape[2]
    for k in range(weak.shape[0]):
        part = arrived[:, :, :, k * width : (k + 1) * width].reshape(tokens, width)
        term = jnp.dot(picked[...], part, preferred_element_type=F32)
        weak[k] = (term if earlier is None else term + earlier[k]).astype(weak.dtype)


def hidden_grads(first, last, rings, w_down, active, slope, picked, dp, *earlier):
    units = active.shape[1]
    quarter = active.shape[0] // len(QUARTERS)
    tokens = (last - first) * quarter
    model = w_down.shape[1]
    parts = parts_of(QUARTERS[first:last])
    pieces = [rings[k][i] for _, i, k, *_ in parts]
    any_ = pl.BlockSpec(memory_space=pl.ANY)
    vmem = pl.BlockSpec(memory_space=pltpu.VMEM)
    flops = 2 * tokens * units * model
    kernel = functools.partial(hidden_kernel, first * quarter, parts)
    if not earlier:
        count = len(pieces) + 4
        kernel = lambda *refs: hidden_kernel(
            first * quarter, parts, *refs[:count], None, *refs[count:]
        )
    return pl.pallas_call(
        kernel,
        in_specs=[any_] * len(pieces) + [vmem] * 4 + [vmem] * len(earlier),
        out_specs=[vmem, vmem],
        out_shape=[
            jax.ShapeDtypeStruct((tokens, 2 * units), BF16),
            jax.ShapeDtypeStruct(
                (dp, picked.shape[0], model // dp), BF16 if earlier else F32
            ),
        ],
        scratch_shapes=[
            pltpu.VMEM((last - first, HALF, quarter // HALF, model), BF16),
            pltpu.SemaphoreType.DMA((len(pieces),)),
        ],
        compiler_params=pltpu.CompilerParams(vmem_limit_bytes=VMEM_LIMIT),
        cost_estimate=pl.CostEstimate(flops=flops, bytes_accessed=8 * 2**20, transcendentals=0),
        name="hidden_grads",
    )(*pieces, w_down, active, slope, picked, *earlier)


def input_kernel(sides, far, early, late, gate_weights, up_weights, _, *refs):
    *pieces, both = refs
    rows, step = pieces[0].shape[1:]
    width = gate_weights.shape[1]
    cut, quarter = early.shape[0], both.shape[0] // X

    @pl.when(pl.program_id(0) == 0)
    def _():
        if far:
            both[...] = late[quarter:]
        else:
            both[:cut] = early[...]
            both[cut:] = late[:quarter]

    term = nt_dot(both[:, :width], gate_weights[...]) + nt_dot(both[:, width:], up_weights[...])
    term = term.astype(BF16).reshape(X, 2, -1, rows, step)
    for k, piece in enumerate(pieces):
        piece[...] = term[sides.index(k // 2), 1 - k % 2]


def input_terms(far, early, late, gate_weights, up_weights, earlier):
    tokens, width = (early.shape[0] + late.shape[0]) // 2, early.shape[1]
    model, units = gate_weights.shape
    shape = (Z // 4, tokens // (X * Z // 2))
    sides = [i for i, half in QUARTERS if half == far]
    weights = pl.BlockSpec((STEP, units), lambda n: (n, 0))
    return pl.pallas_call(
        functools.partial(input_kernel, sides, far),
        grid=(model // STEP,),
        in_specs=[whole(early), whole(late), weights, weights, pl.BlockSpec(memory_space=pl.ANY)],
        out_specs=[pl.BlockSpec((*shape, STEP), lambda n: (0, 0, n))] * (2 * X),
        out_shape=[jax.ShapeDtypeStruct((*shape, model), BF16)] * (2 * X),
        scratch_shapes=[pltpu.VMEM((tokens, width), BF16)],
        compiler_params=pltpu.CompilerParams(vmem_limit_bytes=VMEM_LIMIT),
        cost_estimate=pl.CostEstimate(
            flops=2 * tokens * width * model, bytes_accessed=11 * 2**20, transcendentals=0
        ),
        name="input_terms",
    )(early, late, gate_weights, up_weights, earlier)


def total(*terms):
    return functools.reduce(jnp.add, [t.astype(F32) for t in terms])


def per_device(
    out_grad,
    gate_pre,
    up_pre,
    gate_codes,
    up_codes,
    down_codes,
    gate_scale,
    up_scale,
    down_scale,
    weak_weight,
    weak_index,
):
    rank = lax.axis_index("tensor").astype(jnp.int32)
    place = jnp.stack([rank // Z, rank % Z])
    dp = lax.axis_size("dp")
    weak_index = weak_index.reshape(1, -1)

    mine = out_grad[None]
    blocks = {0: mine}

    def near(ring):
        return jnp.concatenate([blocks[j] for j in ORDER[ring]])

    def over_x(block):
        return [block, shift(block, -1), None, shift(block, 1)]

    up, down = shift(mine, 0, 1), shift(mine, 0, -1)
    blocks |= {7: up, 1: down}
    block = near(RINGS[0])
    rings = [over_x(block)]
    up, down = shift(after(up, block), 0, 1), shift(down, 0, -1)
    blocks |= {6: up, 2: down}
    block = near(RINGS[1])
    rings.append(over_x(block))
    across = shift(after(down, rings[0][1], rings[0][3]), 0, -2)
    up, down = shift(after(up, block), 0, 1), shift(down, 0, -1)
    blocks |= {5: up, 3: down, 4: across}
    rings.append(over_x(after(near(RINGS[2]), rings[1][1], rings[1][3])))
    rings[0][2] = shift(rings[0][3], 1)
    rings[1][2] = shift(rings[1][3], 1)
    w_down = down_weights(down_codes, down_scale, weak_weight, weak_index, rings[1][1])
    w_gate = unpack_weights(gate_codes, gate_scale, rings[1][1])
    active, slope, *picked = factors(place, gate_pre, up_pre, weak_index, rings[0][1])
    w_up = unpack_weights(up_codes, up_scale, rings[0][2])
    rings[2][2] = shift(after(rings[2][1], w_up, w_gate, w_down, active), -1)
    saved = (rings, w_down, active, slope)
    early, weak = hidden_grads(0, EARLY, *saved, picked[0], dp)
    late, weak = hidden_grads(EARLY, len(QUARTERS), *saved, picked[1], dp, weak)
    terms = [input_terms(1, early, late, w_gate, w_up, late)]
    terms.append(input_terms(0, early, late, w_gate, w_up, terms[0][0]))

    def side(i, k):
        return terms[k // 2][2 * i + k % 2]

    def summed(k, earlier=()):
        order = lambda term: after(term, *earlier) if earlier else term
        relay_up, relay_down = shift(order(side(2, k)), 1), shift(order(side(2, k + 1)), -1)
        plain_down, plain_up = shift(order(side(3, k)), -1), shift(order(side(1, k + 1)), 1)
        near_up = total(side(1, k), relay_up).astype(BF16)
        near_down = total(side(3, k + 1), relay_down).astype(BF16)
        first = total(side(0, k), shift(near_up, 1), plain_down)
        second = total(side(0, k + 1), shift(near_down, -1), plain_up)
        term = {j: first[p] for p, j in enumerate(ORDER[PAIRS[k]])}
        term |= {j: second[p] for p, j in enumerate(ORDER[PAIRS[k + 1]])}
        return term, near_up, near_down, plain_up, plain_down

    term, near_up, near_down, plain_up, plain_down = summed(0)
    up, down = term[4].astype(BF16), term[5].astype(BF16)
    up, down = shift(up, 0, 1), shift(down, 0, -1)
    up, down = total(term[3], up).astype(BF16), total(term[6], down).astype(BF16)
    up, down = shift(up, 0, 1), shift(down, 0, -1)
    weak = lax.all_to_all(after(weak, near_up, near_down), "dp", 0, 0, tiled=True)
    term, *_ = summed(2, (plain_up, plain_down))
    up, down = total(term[2], up).astype(BF16), total(term[7], down).astype(BF16)
    up, down = shift(up, 0, 1), shift(down, 0, -1)
    up = shift(total(term[1], up).astype(BF16), 0, 1)
    in_grad = total(term[0], up, down).astype(BF16)
    factor = (gate_pre.shape[0] * dp) ** (-0.5)
    return in_grad, total(*[weak[k] for k in range(dp)]) * factor


def solution(mesh):
    in_specs = (
        P(("dp", "tensor"), None),
        P("dp", "tensor"),
        P("dp", "tensor"),
        P(None, "tensor"),
        P(None, "tensor"),
        P("tensor", None),
        P(None, "tensor"),
        P(None, "tensor"),
        P("tensor", None),
        P("tensor", None),
        P("tensor"),
    )
    out_specs = (P(("dp", "tensor"), None), P("tensor", "dp"))
    return jax.shard_map(
        per_device, mesh=mesh, in_specs=in_specs, out_specs=out_specs, check_vma=False
    )
```
